32 devices in a mesh: member: 2 (over y), lat: 4 (over z), lon: 2 (over x), sub: 2 (over core).
Axes of the slice: x: 2, y: 2, z: 4, core: 2. Of those that a mesh axis runs over, the one named last changes fastest.
Arguments:
- grid_latent: bfloat16 [64, 128, 512], P(('member', 'lat'), 'lon'), parts along dimension 0, may hold values from -6 to 6
- mesh_latent: bfloat16 [4096, 512], P(('member', 'lat', 'lon')), parts along dimension 0, may hold values from -6 to 6
- g2m_sender: int32 [8192], P(('lat', 'lon')), may hold values from 0 to 1151
- g2m_receiver: int32 [8192], P(('lat', 'lon')), may hold values from 0 to 255
- g2m_feature: float32 [4, 8192], P(None, ('lat', 'lon')), may hold values from -5 to 5
- tile_count: int32 [16], P(('lat', 'lon')), may hold values from 1 to 32, as said below
- mesh_send: int32 [512], P(('lat', 'lon')), may hold values from 0 to 255
- m2m_sender: int32 [32768], P(('lat', 'lon')), may hold values from 0 to 319, as said below
- m2m_receiver: int32 [32768], P(('lat', 'lon')), may hold values from 0 to 255
- m2m_feature: float32 [4, 32768], P(None, ('lat', 'lon')), may hold values from -5 to 5
- sender_w: bfloat16 [2, 512, 512], P(None, None, 'sub'), may hold values from -0.25 to 0.25
- receiver_w: bfloat16 [2, 512, 512], P(None, None, 'sub'), may hold values from -0.25 to 0.25
- edge_w: float32 [2, 4, 512], P(None, None, 'sub'), may hold values from -3 to 3
- edge_bias: float32 [2, 512], P(None, 'sub'), may hold values from -4 to 4
- msg_w: bfloat16 [2, 512, 512], P(None, 'sub'), may hold values from -0.25 to 0.25
- node_w: bfloat16 [2, 1024, 512], P(None, None, 'sub'), may hold values from -0.1875 to 0.1875
- node_bias: float32 [2, 512], P(None, 'sub'), may hold values from -4 to 4
- node_out: bfloat16 [2, 512, 512], P(None, 'sub'), may hold values from -0.25 to 0.25
- node_gain: float32 [2, 512], replicated, may hold values from 0.5 to 1.5
Outputs:
- mesh_out: bfloat16 [4096, 512], P(('member', 'lat', 'lon')), parts along dimension 0
The draws below stay inside these ranges and needn't reach their ends.
There are 2 independent parts, one for each index of `member`. The reference program is written for one: setup_inputs(seed, part) draws one part's arguments, and reference() takes and returns one part's arrays. A program takes and returns all parts, laid end to end along the dimension named above; an argument that names none is the same for every part. Nothing has to cross between parts.
Inputs may be any that keep to these rules, and one draw needn't show every extreme that they name: `tile_count`: entries 2 p and 2 p + 1 count the live g2m and m2m tiles of patch p, the first at most 8, the second at most 32; each bound is reached by some patch. `m2m_sender`: a sender below 256 is a node of the patch itself; a sender 256 + p * 8 + c read by patch q has c < 2, or p is a neighbour of q: its latitude band differs by at most one and its longitude band by at most one modulo 2, and p != q.
All inputs are finite; a program needn't handle non-finite values.
Results may differ from the reference program's by a relative error of at most 0.0075.
Values may be sent and summed in bfloat16 or wider, within the bound.
A program may use at most 64 MiB of HBM per device.

```python
import jax
import jax.numpy as jnp
from jax import lax

D = 512
H = 512
GY = 8
GX = 64
HALO = 4
M_DEV = 256
TILE = 128
TILES1 = 8
TILES2 = 32
CAP = 8
FAR = 2
BANDS = 4
LONS = 2
PATCHES = 8
NY = 32
NX = 128
NM = 2048
E1 = 1024
E2 = 4096


def draw_tile_count(key, part):
    key = jax.random.fold_in(key, 11)
    band_index = jnp.arange(PATCHES, dtype=jnp.int32) // LONS
    distance = jnp.abs(2 * band_index - BANDS + 1)
    first_jitter = jax.random.randint(jax.random.fold_in(key, 0), (PATCHES,), 0, 2)
    first_jitter = jnp.where(distance == 1, 0, first_jitter)
    first_count = jnp.clip(TILES1 - first_jitter, 1, TILES1)
    base_count = TILES2 - (distance - 1) * (TILES2 - 1) // max(BANDS - 2, 1)
    second_jitter = jax.random.randint(jax.random.fold_in(key, 1), (PATCHES,), -1, 2)
    second_jitter = jnp.where(distance == 1, 0, second_jitter)
    second_count = jnp.clip(base_count + second_jitter, 1, TILES2)
    second_count = jnp.where(distance == 1, TILES2, second_count)
    return jnp.stack([first_count, second_count], axis=1).reshape(-1).astype(jnp.int32)


def draw_m2m_sender(key, part):
    key = jax.random.fold_in(key, 23)
    shape = (PATCHES * E2,)
    flat = jnp.arange(PATCHES * E2, dtype=jnp.int32)
    patch = flat // E2
    slot = flat % E2
    band = patch // LONS
    lon_band = patch % LONS
    kind = jax.random.randint(jax.random.fold_in(key, 0), shape, 0, 100)
    own_row = jax.random.randint(jax.random.fold_in(key, 1), shape, 0, M_DEV)
    direction = jax.random.randint(jax.random.fold_in(key, 2), shape, 0, 8)
    forced_near = (slot >= 1) & (slot <= 8)
    direction = jnp.where(forced_near, slot - 1, direction)
    code = direction + (direction >= 4).astype(jnp.int32)
    delta_lat = code // 3 - 1
    delta_lon = code % 3 - 1
    near_band = band + delta_lat
    near_band = jnp.where((near_band < 0) | (near_band >= BANDS), band - delta_lat, near_band)
    near_patch = near_band * LONS + (lon_band + delta_lon + LONS) % LONS
    near_pos = jax.random.randint(jax.random.fold_in(key, 3), shape, FAR, CAP)
    far_patch = jax.random.randint(jax.random.fold_in(key, 4), shape, 0, PATCHES)
    far_patch = jnp.where(slot == 0, (patch + PATCHES // 2) % PATCHES, far_patch)
    far_pos = jax.random.randint(jax.random.fold_in(key, 5), shape, 0, FAR)
    near_row = M_DEV + near_patch * CAP + near_pos
    far_row = M_DEV + far_patch * CAP + far_pos
    is_far = (slot == 0) | (kind >= 97) & (slot > 9)
    is_near = forced_near | (kind >= 80) & (kind < 97) & (slot > 9)
    result = jnp.where(is_far, far_row, jnp.where(is_near, near_row, own_row))
    result = jnp.where((patch == 0) & (slot == 9), 0, result)
    result = jnp.where((patch == PATCHES - 2) & (slot == 9), M_DEV + (PATCHES - 1) * CAP + CAP - 1, result)
    return result.astype(jnp.int32)


def set_ends(entries, own_key, least, top_value):
    longest = entries.shape.index(max(entries.shape))
    spots = []
    for shift in (0, 1):
        where = [jax.random.randint(jax.random.fold_in(own_key, axis), (), 0, length) for axis, length in enumerate(entries.shape)]
        where[longest] = (where[longest] + shift) % entries.shape[longest]
        spots.append(tuple(where))
    return entries.at[spots[0]].set(least).at[spots[1]].set(top_value)


def levels(stream_key, shape, pieces, least, largest):
    def one(axis_at, blocks):
        steps = jax.random.uniform(jax.random.fold_in(jax.random.fold_in(stream_key, 6), axis_at), (blocks,), jnp.float32, least / len(pieces), largest / len(pieces))
        return jnp.repeat(jnp.exp(steps), shape[axis_at] // blocks).reshape((-1,) + (1,) * (len(shape) - axis_at - 1))

    loudness = one(*pieces[0])
    for cut in pieces[1:]:
        loudness = loudness * one(*cut)
    return loudness


def scatter_about(stream_key, dims, deviation, reach, cuts=(), kind=jnp.bfloat16):
    entries = deviation * jax.random.normal(stream_key, dims, jnp.float32)
    if cuts:
        entries = entries * levels(stream_key, dims, cuts, -0.22, 0.18)
    return jnp.clip(entries, -reach, reach).astype(kind)


def setup_inputs(seed: int = 0, part: int = 0) -> dict:
    streams_of = jax.random.split(jax.random.key(seed), 20)
    part_keys = jax.random.split(jax.random.fold_in(streams_of[19], part), 20)
    return {
        "grid_latent": scatter_about(part_keys[0], (NY, NX, D), 1.0, 6.0, ((0, 4), (1, 2))),
        "mesh_latent": scatter_about(part_keys[1], (NM, D), 1.0, 6.0, ((0, 8),)),
        "g2m_sender": set_ends(jax.random.randint(streams_of[2], (PATCHES * E1,), 0, (GY + 2 * HALO) * (GX + 2 * HALO)), jax.random.fold_in(streams_of[2], 1), 0, ((GY + 2 * HALO) * (GX + 2 * HALO)) - 1).astype(jnp.int32),
        "g2m_receiver": set_ends(jax.random.randint(streams_of[3], (PATCHES * E1,), 0, M_DEV), jax.random.fold_in(streams_of[3], 1), 0, M_DEV - 1).astype(jnp.int32),
        "g2m_feature": scatter_about(streams_of[4], (4, PATCHES * E1), 1.0, 5.0, ((1, 8),), jnp.float32),
        "tile_count": draw_tile_count(jax.random.fold_in(streams_of[19], 71), part),
        "mesh_send": set_ends(jax.random.randint(streams_of[6], (PATCHES * PATCHES * CAP,), 0, M_DEV), jax.random.fold_in(streams_of[6], 1), 0, M_DEV - 1).astype(jnp.int32),
        "m2m_sender": draw_m2m_sender(jax.random.fold_in(streams_of[19], 71), part),
        "m2m_receiver": set_ends(jax.random.randint(streams_of[8], (PATCHES * E2,), 0, M_DEV), jax.random.fold_in(streams_of[8], 1), 0, M_DEV - 1).astype(jnp.int32),
        "m2m_feature": scatter_about(streams_of[9], (4, PATCHES * E2), 1.0, 5.0, ((1, 8),), jnp.float32),
        "sender_w": scatter_about(streams_of[10], (2, D, H), D ** -0.5, 0.25, ((2, 2),)),
        "receiver_w": scatter_about(streams_of[11], (2, D, H), D ** -0.5, 0.25, ((2, 2),)),
        "edge_w": scatter_about(streams_of[12], (2, 4, H), 4 ** -0.5, 3.0, ((2, 2),), jnp.float32),
        "edge_bias": scatter_about(streams_of[13], (2, H), 1.0, 4.0, ((1, 2),), jnp.float32),
        "msg_w": scatter_about(streams_of[14], (2, H, D), H ** -0.5, 0.25, ((1, 2),)),
        "node_w": scatter_about(streams_of[15], (2, 2 * D, H), (2 * D) ** -0.5, 0.1875, ((2, 2),)),
        "node_bias": scatter_about(streams_of[16], (2, H), 1.0, 4.0, ((1, 2),), jnp.float32),
        "node_out": scatter_about(streams_of[17], (2, H, D), H ** -0.5, 0.25, ((1, 2),)),
        "node_gain": jnp.clip(1.0 + 0.1 * jax.random.normal(streams_of[18], (2, D), jnp.float32), 0.5, 1.5),
    }


def layer_norm(values):
    average = lax.optimization_barrier(jnp.mean(values, axis=-1, keepdims=True))
    centred = values - average
    variance = lax.optimization_barrier(jnp.mean(centred * centred, axis=-1, keepdims=True))
    return centred * lax.rsqrt(variance + 1e-05)

def edge_block(window, recv_proj, senders, receivers, features, live_mask, edge_weight, edge_offset, msg_weight):
    preact = window[senders].astype(jnp.float32) + recv_proj[receivers]
    preact = preact + jnp.dot(features.T, edge_weight, precision=lax.Precision.HIGHEST, preferred_element_type=jnp.float32) + edge_offset
    hidden = jax.nn.silu(preact).astype(jnp.bfloat16)
    messages = jnp.dot(hidden, msg_weight, preferred_element_type=jnp.float32)
    messages = jnp.where(live_mask[:, None], messages, jnp.float32(0.0))
    return jnp.zeros((M_DEV, msg_weight.shape[1]), jnp.float32).at[receivers].add(messages)

def node_update(latent, inbound, node_weight, node_offset, out_weight, gain_row):
    joined = jnp.concatenate([latent, inbound.astype(jnp.bfloat16)], axis=1)
    hidden = jax.nn.silu(jnp.dot(joined, node_weight, preferred_element_type=jnp.float32) + node_offset).astype(jnp.bfloat16)
    node_sum = jnp.dot(hidden, out_weight, preferred_element_type=jnp.float32)
    return (latent.astype(jnp.float32) + layer_norm(node_sum) * gain_row).astype(jnp.bfloat16)

def reference(grid_latent, mesh_latent, g2m_sender, g2m_receiver, g2m_feature, tile_count, mesh_send, m2m_sender, m2m_receiver, m2m_feature, sender_w, receiver_w, edge_w, edge_bias, msg_w, node_w, node_bias, node_out, node_gain):
    sender_grid = jnp.dot(grid_latent.reshape(NY * NX, D), sender_w[0], preferred_element_type=jnp.float32)
    sender_grid = sender_grid.astype(jnp.bfloat16).reshape(NY, NX, H)
    wrapped = jnp.concatenate([sender_grid[:, NX - HALO:], sender_grid, sender_grid[:, :HALO]], axis=1)
    padded = jnp.pad(wrapped, ((HALO, HALO), (0, 0), (0, 0)))
    counts = tile_count.reshape(PATCHES, 2)
    receiver_mesh = jnp.dot(mesh_latent, receiver_w[0], preferred_element_type=jnp.float32).reshape(PATCHES, M_DEV, H)
    first_tiles = jnp.arange(E1, dtype=jnp.int32) // TILE
    second_tiles = jnp.arange(E2, dtype=jnp.int32) // TILE

    def encode(patch_id):
        band_row = patch_id // LONS * GY
        band_col = patch_id % LONS * GX
        window = lax.dynamic_slice(padded, (band_row, band_col, jnp.int32(0)), (GY + 2 * HALO, GX + 2 * HALO, H)).reshape(-1, H)
        senders = lax.dynamic_slice_in_dim(g2m_sender, patch_id * E1, E1)
        receivers = lax.dynamic_slice_in_dim(g2m_receiver, patch_id * E1, E1)
        features = lax.dynamic_slice_in_dim(g2m_feature, patch_id * E1, E1, 1)
        live_mask = first_tiles < counts[patch_id, 0]
        return edge_block(window, receiver_mesh[patch_id], senders, receivers, features, live_mask, edge_w[0], edge_bias[0], msg_w[0])
    inbound = lax.map(encode, jnp.arange(PATCHES, dtype=jnp.int32)).reshape(NM, D)
    mesh_mid = node_update(mesh_latent, inbound, node_w[0], node_bias[0], node_out[0], node_gain[0])
    sender_mesh = jnp.dot(mesh_mid, sender_w[1], preferred_element_type=jnp.float32).astype(jnp.bfloat16).reshape(PATCHES, M_DEV, H)
    receiver_mid = jnp.dot(mesh_mid, receiver_w[1], preferred_element_type=jnp.float32).reshape(PATCHES, M_DEV, H)
    send_lists = mesh_send.reshape(PATCHES, PATCHES, CAP)
    sources = jnp.arange(PATCHES, dtype=jnp.int32)[:, None]

    def process(patch_id):
        received = sender_mesh[sources, send_lists[:, patch_id, :]].reshape(PATCHES * CAP, H)
        sender_table = jnp.concatenate([sender_mesh[patch_id], received], axis=0)
        senders = lax.dynamic_slice_in_dim(m2m_sender, patch_id * E2, E2)
        receivers = lax.dynamic_slice_in_dim(m2m_receiver, patch_id * E2, E2)
        features = lax.dynamic_slice_in_dim(m2m_feature, patch_id * E2, E2, 1)
        live_mask = second_tiles < counts[patch_id, 1]
        return edge_block(sender_table, receiver_mid[patch_id], senders, receivers, features, live_mask, edge_w[1], edge_bias[1], msg_w[1])
    inbound_mid = lax.map(process, jnp.arange(PATCHES, dtype=jnp.int32)).reshape(NM, D)
    return node_update(mesh_mid, inbound_mid, node_w[1], node_bias[1], node_out[1], node_gain[1])
```

```python
import functools

import jax
import jax.numpy as jnp
from jax import lax
from jax.experimental import pallas as pl
from jax.experimental.pallas import tpu as pltpu
from jax.sharding import PartitionSpec as P

HALO = 4
TILE = 128
FEAT_ROWS = 16
MESH = pl.DeviceIdType.MESH
BF = jnp.bfloat16
F32 = jnp.float32


def dot(a, b):
    return lax.dot_general(a, b, (((1,), (0,)), ((), ())), preferred_element_type=F32)


def dot_tn(a, b):
    return lax.dot_general(a, b, (((0,), (0,)), ((), ())), preferred_element_type=F32)


def dot_nt(a, b):
    return lax.dot_general(a, b, (((1,), (1,)), ((), ())), preferred_element_type=F32)


def silu(v):
    h = 0.5 * v
    return h + h * jnp.tanh(h)


def one_hot(ids, rows, first=0):
    numbers = lax.broadcasted_iota(jnp.int32, (rows, ids.shape[1]), 0) + first
    return jnp.where(numbers == ids, 1.0, 0.0).astype(BF)


def split(v):
    high = v.astype(BF).astype(F32)
    return high, v - high


def layer_norm(values):
    average = jnp.mean(values, axis=-1, keepdims=True)
    centred = values - average
    variance = jnp.mean(centred * centred, axis=-1, keepdims=True)
    return centred * lax.rsqrt(variance + 1e-05)


def kernel(
    dims,
    grid_h, mesh_h, snd1_h, rcv1_h, feat1_h, tiles_h, lists_h, snd2_h, rcv2_h, feat2_h,
    sw_h, rw_h, ew_h, eb_h, mw_h, nw_h, nb_h, no_h, gain_h,
    out_ref,
    grid, mesh, snd1, rcv1, feat1, tiles, lists, snd2, rcv2, feat2,
    sw, rw, ew, eb, mw, nw, nb, no, gain,
    table1, halo, pack, hot1, hot1h, pre1, fs1,
    table2, listed, arrived, hot2, hot2l, pre2, fs2, wf,
    sums, local_sem, weight_send, weight_recv, halo_send, halo_recv, sum_send, sum_recv,
    list_send, list_recv,
):
    bands, lons, gy, gx, cap = dims
    patches = bands * lons
    lat, lon, sub = lax.axis_index("lat"), lax.axis_index("lon"), lax.axis_index("sub")
    me = lat * lons + lon
    peer = {"sub": 1 - sub}
    cells = gy * gx
    nodes = mesh.shape[0]
    edges1, edges2 = snd1.shape[1], snd2.shape[1]

    pairs = [
        (grid_h, grid), (sw_h.at[0], sw.at[0]), (mesh_h, mesh), (rw_h.at[0], rw.at[0]),
        (snd1_h, snd1), (rcv1_h, rcv1), (feat1_h, feat1), (tiles_h, tiles), (ew_h, ew), (eb_h, eb),
        (snd2_h, snd2), (rcv2_h, rcv2), (feat2_h, feat2), (lists_h, lists),
        (mw_h.at[0], mw.at[0, sub]), (nw_h.at[0], nw.at[0, sub]), (nb_h, nb.at[sub]),
        (no_h.at[0], no.at[0, sub]), (gain_h, gain),
        (sw_h.at[1], sw.at[1]), (rw_h.at[1], rw.at[1]),
        (mw_h.at[1], mw.at[1, sub]), (nw_h.at[1], nw.at[1, sub]), (no_h.at[1], no.at[1, sub]),
    ]
    local = [pltpu.make_async_copy(s, d, local_sem.at[i]) for i, (s, d) in enumerate(pairs)]
    for copy in local:
        copy.start()

    barrier = pltpu.get_barrier_semaphore()
    pl.semaphore_signal(barrier, inc=1, device_id=peer, device_id_type=MESH)
    for k in range(1, patches):
        q = lax.rem(me + k, patches)
        pl.semaphore_signal(
            barrier, inc=1, device_id={"lat": q // lons, "lon": lax.rem(q, lons)}, device_id_type=MESH
        )

    for i in (0, 1):
        local[i].wait()
    table1[0:cells, :] = dot(grid[...], sw[0]).astype(BF)
    side = gy * HALO
    row = lax.broadcasted_iota(jnp.int32, (2 * side, cells), 0)
    col = lax.broadcasted_iota(jnp.int32, (2 * side, cells), 1)
    within = lax.rem(row, side)
    wanted = (within // HALO) * gx + lax.rem(within, HALO) + jnp.where(row >= side, gx - HALO, 0)
    choose = jnp.where(col == wanted, 1.0, 0.0).astype(BF)
    pack[...] = dot(choose, table1[0:cells, :]).astype(BF)

    pl.semaphore_wait(barrier, patches)

    strip = HALO * gx
    half = HALO * HALO
    west = lax.rem(lon + lons - 1, lons)
    east = lax.rem(lon + 1, lons)
    base = 2 * strip
    has_n, has_s = lat > 0, lat < bands - 1

    def halo_copy(i, src, dst, where):
        return pltpu.make_async_remote_copy(
            src_ref=src, dst_ref=halo.at[pl.ds(dst[0], dst[1])], send_sem=halo_send.at[i],
            recv_sem=halo_recv.at[i], device_id=where, device_id_type=MESH,
        )

    north = [
        halo_copy(0, table1.at[pl.ds(0, strip)], (strip, strip), {"lat": lat - 1}),
        halo_copy(1, pack.at[pl.ds(0, half)], (base + 2 * side + 3 * half, half), {"lat": lat - 1, "lon": west}),
        halo_copy(2, pack.at[pl.ds(side, half)], (base + 2 * side + 2 * half, half), {"lat": lat - 1, "lon": east}),
    ]
    south = [
        halo_copy(3, table1.at[pl.ds(cells - strip, strip)], (0, strip), {"lat": lat + 1}),
        halo_copy(4, pack.at[pl.ds(side - half, half)], (base + 2 * side + half, half), {"lat": lat + 1, "lon": west}),
        halo_copy(5, pack.at[pl.ds(2 * side - half, half)], (base + 2 * side, half), {"lat": lat + 1, "lon": east}),
    ]
    across = [
        halo_copy(6, pack.at[pl.ds(0, side)], (base + side, side), {"lon": west}),
        halo_copy(7, pack.at[pl.ds(side, side)], (base, side), {"lon": east}),
    ]

    @pl.when(has_n)
    def _():
        for copy in north:
            copy.start()

    @pl.when(has_s)
    def _():
        for copy in south:
            copy.start()

    for copy in across:
        copy.start()

    weights = [
        pltpu.make_async_remote_copy(
            src_ref=s, dst_ref=d, send_sem=weight_send.at[i], recv_sem=weight_recv.at[i],
            device_id=peer, device_id_type=MESH,
        )
        for i, (s, d) in enumerate(
            [
                (mw_h.at[0], mw.at[0, sub]), (nw_h.at[0], nw.at[0, sub]), (nb_h, nb.at[sub]),
                (no_h.at[0], no.at[0, sub]),
                (mw_h.at[1], mw.at[1, sub]), (nw_h.at[1], nw.at[1, sub]), (no_h.at[1], no.at[1, sub]),
            ]
        )
    ]
    for copy in weights:
        copy.start()

    @pl.when(jnp.logical_not(has_n))
    def _():
        halo[0:strip, :] = jnp.zeros((strip, halo.shape[1]), BF)
        halo[base + 2 * side:base + 2 * side + 2 * half, :] = jnp.zeros((2 * half, halo.shape[1]), BF)

    @pl.when(jnp.logical_not(has_s))
    def _():
        halo[strip:base, :] = jnp.zeros((strip, halo.shape[1]), BF)
        halo[base + 2 * side + 2 * half:base + 2 * side + 4 * half, :] = jnp.zeros(
            (2 * half, halo.shape[1]), BF
        )

    for i in range(2, 14):
        local[i].wait()
    table1[cells:cells + nodes, :] = dot(mesh[...], rw[0]).astype(BF)

    def weight_rows(layer):
        high, low = split(ew[layer])
        wf[0:4, :] = high
        wf[4:8, :] = high
        wf[8:12, :] = low
        high, low = split(eb[pl.ds(layer, 1), :])
        wf[12:13, :] = high
        wf[13:14, :] = low
        wf[14:16, :] = jnp.zeros((2, wf.shape[1]), F32)
        return wf[...].astype(BF)

    def feature_rows(fs, feat):
        high, low = split(feat[...])
        fs[0:4, :] = high
        fs[4:8, :] = low
        fs[8:12, :] = high
        fs[12:16, :] = jnp.ones((4, fs.shape[1]), F32)
        return fs[...].astype(BF)

    table1[cells + nodes:cells + nodes + FEAT_ROWS, :] = weight_rows(0)
    hot1[cells + nodes:cells + nodes + FEAT_ROWS, :] = feature_rows(fs1, feat1)

    def live(ids, which):
        slot = lax.broadcasted_iota(jnp.int32, ids.shape, 1)
        return jnp.where(slot < tiles[0:1, which:which + 1] * TILE, ids, -1)

    wide = gx + 2 * HALO
    place = snd1[...]
    r = place // wide
    c = place - r * wide
    rr, cc = r - HALO, c - HALO
    inside = (cc >= 0) & (cc < gx)
    edge_col = jnp.where(cc < 0, c, cc - gx)
    far_side = jnp.where(cc < 0, 0, 1)
    middle = jnp.where(inside, rr * gx + cc, cells + base + far_side * side + rr * HALO + edge_col)
    upper = jnp.where(inside, cells + r * gx + cc, cells + base + 2 * side + far_side * half + r * HALO + edge_col)
    down = rr - gy
    lower = jnp.where(
        inside,
        cells + strip + down * gx + cc,
        cells + base + 2 * side + (2 + far_side) * half + down * HALO + edge_col,
    )
    place = jnp.where(rr < 0, upper, jnp.where(rr >= gy, lower, middle))
    hot1[0:cells, :] = one_hot(place, cells)
    hot1h[...] = one_hot(place, hot1h.shape[0], cells)
    hot1[cells:cells + nodes, :] = one_hot(live(rcv1[...], 0), nodes)
    pre1[...] = dot_tn(table1[...], hot1[...])

    hot2[2 * nodes:2 * nodes + FEAT_ROWS, :] = feature_rows(fs2, feat2)
    rcv2[...] = live(rcv2[...], 1)
    span = min(512, edges2)

    def select(step, carry):
        at = pl.ds(pl.multiple_of(step * span, span), span)
        ids = snd2[:, at]
        hot2[0:nodes, at] = one_hot(ids, nodes)
        hot2[nodes:2 * nodes, at] = one_hot(rcv2[:, at], nodes)
        source = (ids - nodes) // cap
        turn = me - source
        turn = jnp.where(turn < 0, turn + patches, turn)
        ids = jnp.where(ids < nodes, -1, turn * cap + (ids - nodes) - source * cap)
        hot2l[:, at] = one_hot(ids, patches * cap)
        return carry

    lax.fori_loop(0, edges2 // span, select, 0)

    @pl.when(has_n)
    def _():
        for i in (3, 4, 5):
            south[i - 3].wait_recv()
        for copy in north:
            copy.wait_send()

    @pl.when(has_s)
    def _():
        for copy in north:
            copy.wait_recv()
        for copy in south:
            copy.wait_send()

    for copy in across:
        copy.wait()
    hidden = silu(pre1[...] + dot_tn(halo[...], hot1h[...])).astype(BF)

    def exchange(layer, total):
        sums[layer, sub] = total.astype(BF)
        copy = pltpu.make_async_remote_copy(
            src_ref=sums.at[layer, sub], dst_ref=sums.at[layer, sub], send_sem=sum_send.at[layer],
            recv_sem=sum_recv.at[layer], device_id=peer, device_id_type=MESH,
        )
        copy.start()
        return copy

    def node_update(latent, layer):
        inbound = dot(sums[layer, 0], mw[layer, 0]) + dot(sums[layer, 1], mw[layer, 1])
        joined = jnp.concatenate([latent, inbound.astype(BF)], axis=1)
        total = 0.0
        for j in (0, 1):
            units = silu(dot(joined, nw[layer, j]) + nb[j, layer:layer + 1, :]).astype(BF)
            total = total + dot(units, no[layer, j])
        return (latent.astype(F32) + layer_norm(total) * gain[layer:layer + 1, :]).astype(BF)

    copy = exchange(0, dot_nt(hot1[cells:cells + nodes, :], hidden))
    table2[2 * nodes:2 * nodes + FEAT_ROWS, :] = weight_rows(1)
    for i in range(14, len(local)):
        local[i].wait()
    for other in weights[:4]:
        other.wait()
    copy.wait()
    mid = node_update(mesh[...], 0)

    sender = dot(mid, sw[1]).astype(BF)
    table2[0:nodes, :] = sender
    listed[...] = dot_tn(one_hot(lists[...], nodes), sender).reshape(listed.shape)
    routes = []
    for k in range(1, patches):
        q = lax.rem(me + k, patches)
        routes.append(
            pltpu.make_async_remote_copy(
                src_ref=listed.at[q], dst_ref=arrived.at[k], send_sem=list_send.at[k],
                recv_sem=list_recv.at[k], device_id={"lat": q // lons, "lon": lax.rem(q, lons)},
                device_id_type=MESH,
            )
        )
        routes[-1].start()
    arrived[0] = listed[me]
    table2[nodes:2 * nodes, :] = dot(mid, rw[1]).astype(BF)

    def before(step, carry):
        at = pl.ds(pl.multiple_of(step * span, span), span)
        pre2[:, at] = dot_tn(table2[...], hot2[:, at])
        return carry

    lax.fori_loop(0, edges2 // span, before, 0)
    for route in routes:
        route.wait()
    far = arrived[...].reshape(patches * cap, arrived.shape[2]).astype(BF)

    def after(step, total):
        at = pl.ds(pl.multiple_of(step * span, span), span)
        hidden = silu(pre2[:, at] + dot_tn(far, hot2l[:, at])).astype(BF)
        return total + dot_nt(hot2[nodes:2 * nodes, at], hidden)

    total = lax.fori_loop(0, edges2 // span, after, jnp.zeros((nodes, far.shape[1]), F32))
    copy = exchange(1, total)
    for other in weights[4:]:
        other.wait()
    copy.wait()
    out_ref[...] = node_update(mid, 1)


def body(*args):
    (grid, mesh, snd1, rcv1, feat1, tiles, lists, snd2, rcv2, feat2,
     sw, rw, ew, eb, mw, nw, nb, no, gain) = args
    gy, gx, width = grid.shape
    bands, lons = lax.axis_size("lat"), lax.axis_size("lon")
    patches = bands * lons
    nodes = mesh.shape[0]
    units = sw.shape[2]
    cap = lists.shape[0] // patches
    edges1, edges2 = snd1.shape[0], snd2.shape[0]
    cells = gy * gx
    ring = (gy + 2 * HALO) * (gx + 2 * HALO) - cells
    operands = [
        grid.reshape(cells, width), mesh, snd1.reshape(1, -1), rcv1.reshape(1, -1), feat1,
        tiles.reshape(1, -1), lists.reshape(1, -1), snd2.reshape(1, -1), rcv2.reshape(1, -1), feat2,
        sw, rw, ew, eb, mw, nw, nb, no, gain,
    ]
    shapes = [op.shape for op in operands]
    for i in (14, 15, 17):
        shapes[i] = (shapes[i][0], 2) + shapes[i][1:]
    shapes[16] = (2,) + shapes[16]
    held = [pltpu.VMEM(shape, op.dtype) for shape, op in zip(shapes, operands)]
    dma = pltpu.SemaphoreType.DMA
    scratch = held + [
        pltpu.VMEM((cells + nodes + FEAT_ROWS, units), BF),
        pltpu.VMEM((ring, units), BF),
        pltpu.VMEM((2 * gy * HALO, units), BF),
        pltpu.VMEM((cells + nodes + FEAT_ROWS, edges1), BF),
        pltpu.VMEM((ring, edges1), BF),
        pltpu.VMEM((units, edges1), F32),
        pltpu.VMEM((FEAT_ROWS, edges1), F32),
        pltpu.VMEM((2 * nodes + FEAT_ROWS, units), BF),
        pltpu.VMEM((patches, cap, units), F32),
        pltpu.VMEM((patches, cap, units), F32),
        pltpu.VMEM((2 * nodes + FEAT_ROWS, edges2), BF),
        pltpu.VMEM((patches * cap, edges2), BF),
        pltpu.VMEM((units, edges2), F32),
        pltpu.VMEM((FEAT_ROWS, edges2), F32),
        pltpu.VMEM((FEAT_ROWS, units), F32),
        pltpu.VMEM((2, 2, nodes, units), BF),
        dma((24,)), dma((7,)), dma((7,)), dma((8,)), dma((8,)), dma((2,)), dma((2,)),
        dma((patches,)), dma((patches,)),
    ]
    return pl.pallas_call(
        functools.partial(kernel, (bands, lons, gy, gx, cap)),
        out_shape=jax.ShapeDtypeStruct(mesh.shape, mesh.dtype),
        in_specs=[pl.BlockSpec(memory_space=pl.ANY)] * len(operands),
        out_specs=pl.BlockSpec(memory_space=pltpu.VMEM),
        scratch_shapes=scratch,
        compiler_params=pltpu.CompilerParams(
            collective_id=0, has_side_effects=True, vmem_limit_bytes=58 * 1024 * 1024
        ),
        name="encoder_processor",
    )(*operands)


def solution(mesh):
    placed = (
        P(("member", "lat"), "lon", None),
        P(("member", "lat", "lon"), None),
        P(("lat", "lon")),
        P(("lat", "lon")),
        P(None, ("lat", "lon")),
        P(("lat", "lon")),
        P(("lat", "lon")),
        P(("lat", "lon")),
        P(("lat", "lon")),
        P(None, ("lat", "lon")),
        P(None, None, "sub"),
        P(None, None, "sub"),
        P(None, None, "sub"),
        P(None, "sub"),
        P(None, "sub", None),
        P(None, None, "sub"),
        P(None, "sub"),
        P(None, "sub", None),
        P(),
    )
    return jax.shard_map(
        body,
        mesh=mesh,
        in_specs=placed,
        out_specs=P(("member", "lat", "lon"), None),
        check_vma=False,
    )
```

```python
import functools

import jax
import jax.numpy as jnp
from jax import lax
from jax.experimental import pallas as pl
from jax.experimental.pallas import tpu as pltpu
from jax.sharding import PartitionSpec as P

HALO = 4
TILE = 128
SPAN = 512
FEAT_ROWS = 16
MESH = pl.DeviceIdType.MESH
BF = jnp.bfloat16
F32 = jnp.float32


def dot(a, b):
    return lax.dot_general(a, b, (((1,), (0,)), ((), ())), preferred_element_type=F32)


def dot_tn(a, b):
    return lax.dot_general(a, b, (((0,), (0,)), ((), ())), preferred_element_type=F32)


def dot_nt(a, b):
    return lax.dot_general(a, b, (((1,), (1,)), ((), ())), preferred_element_type=F32)


def silu(v):
    h = 0.5 * v
    return h + h * jnp.tanh(h)


def one_hot(ids, rows, first=0):
    numbers = lax.broadcasted_iota(jnp.int32, (rows, ids.shape[1]), 0) + first
    return jnp.where(numbers == ids, 1.0, 0.0).astype(BF)


def split(v):
    high = v.astype(BF).astype(F32)
    return high, v - high


def layer_norm(values):
    average = jnp.mean(values, axis=-1, keepdims=True)
    centred = values - average
    variance = jnp.mean(centred * centred, axis=-1, keepdims=True)
    return centred * lax.rsqrt(variance + 1e-05)


def kernel(
    dims,
    grid_h, mesh_h, snd1_h, rcv1_h, feat1_h, tiles_h, lists_h, snd2_h, rcv2_h, feat2_h,
    sw_h, rw_h, ew_h, eb_h, mw_h, nw_h, nb_h, no_h, gain_h,
    out_ref,
    grid, mesh, snd1, rcv1, feat1, tiles, lists, snd2, rcv2, feat2,
    sw, rw, ew, eb, mw, nw, nb, no, gain,
    table1, halo, pack, hot1, hot1h, pre1, fs1,
    table2, listed, arrived, hot2, hot2f, hot2l, pre2, fs2, wf,
    sums, fixed, relay, local_sem, weight_send, weight_recv, halo_send, halo_recv, sum_send, sum_recv,
    list_send, list_recv,
):
    bands, lons, gy, gx, cap = dims
    patches = bands * lons
    lat, lon, sub = lax.axis_index("lat"), lax.axis_index("lon"), lax.axis_index("sub")
    me = lat * lons + lon
    peer = {"sub": 1 - sub}
    cells = gy * gx
    nodes = mesh.shape[0]
    edges1, edges2 = snd1.shape[1], snd2.shape[1]

    pairs = [
        (grid_h, grid), (sw_h.at[0], sw.at[0]), (mesh_h, mesh), (rw_h.at[0], rw.at[0]),
        (snd1_h, snd1), (rcv1_h, rcv1), (feat1_h, feat1), (tiles_h, tiles), (ew_h, ew), (eb_h, eb),
        (snd2_h, snd2), (rcv2_h, rcv2), (feat2_h, feat2), (lists_h, lists),
        (mw_h.at[0], mw.at[0, sub]), (nw_h.at[0], nw.at[0, sub]), (nb_h, nb.at[sub]),
        (no_h.at[0], no.at[0, sub]), (gain_h, gain),
        (sw_h.at[1], sw.at[1]), (rw_h.at[1], rw.at[1]),
        (mw_h.at[1], mw.at[1, sub]), (nw_h.at[1], nw.at[1, sub]), (no_h.at[1], no.at[1, sub]),
    ]
    local = [pltpu.make_async_copy(s, d, local_sem.at[i]) for i, (s, d) in enumerate(pairs)]
    for copy in local[:14]:
        copy.start()

    turns = (0, 1) if lons == 2 else (0, 1, lons - 1)
    has_n, has_s = lat > 0, lat < bands - 1
    around = len(turns) - 1 + len(turns) * (has_n.astype(jnp.int32) + has_s.astype(jnp.int32))

    def greet(sem):
        for turn in turns[1:]:
            pl.semaphore_signal(
                sem, inc=1, device_id={"lon": lax.rem(lon + turn, lons)}, device_id_type=MESH
            )
        for there, shift in ((has_n, -1), (has_s, 1)):

            @pl.when(there)
            def _():
                for turn in turns:
                    pl.semaphore_signal(
                        sem, inc=1, device_id={"lat": lat + shift, "lon": lax.rem(lon + turn, lons)},
                        device_id_type=MESH,
                    )

    barrier = pltpu.get_barrier_semaphore()
    pl.semaphore_signal(barrier, inc=1, device_id=peer, device_id_type=MESH)
    greet(barrier)
    rounds = max(bands - 2, lons // 2 - 1)

    for i in (0, 1):
        local[i].wait()
    table1[0:cells, :] = dot(grid[...], sw[0]).astype(BF)
    side = gy * HALO
    row = lax.broadcasted_iota(jnp.int32, (2 * side, cells), 0)
    col = lax.broadcasted_iota(jnp.int32, (2 * side, cells), 1)
    within = lax.rem(row, side)
    wanted = (within // HALO) * gx + lax.rem(within, HALO) + jnp.where(row >= side, gx - HALO, 0)
    choose = jnp.where(col == wanted, 1.0, 0.0).astype(BF)
    pack[...] = dot(choose, table1[0:cells, :]).astype(BF)

    for copy in local[14:]:
        copy.start()
    pl.semaphore_wait(barrier, around + 1)

    strip = HALO * gx
    half = HALO * HALO
    west = lax.rem(lon + lons - 1, lons)
    east = lax.rem(lon + 1, lons)
    base = 2 * strip
    def halo_copy(i, src, dst, where):
        return pltpu.make_async_remote_copy(
            src_ref=src, dst_ref=halo.at[pl.ds(dst[0], dst[1])], send_sem=halo_send.at[i],
            recv_sem=halo_recv.at[i], device_id=where, device_id_type=MESH,
        )

    north = [
        halo_copy(0, table1.at[pl.ds(0, strip)], (strip, strip), {"lat": lat - 1}),
        halo_copy(1, pack.at[pl.ds(0, half)], (base + 2 * side + 3 * half, half), {"lat": lat - 1, "lon": west}),
        halo_copy(2, pack.at[pl.ds(side, half)], (base + 2 * side + 2 * half, half), {"lat": lat - 1, "lon": east}),
    ]
    south = [
        halo_copy(3, table1.at[pl.ds(cells - strip, strip)], (0, strip), {"lat": lat + 1}),
        halo_copy(4, pack.at[pl.ds(side - half, half)], (base + 2 * side + half, half), {"lat": lat + 1, "lon": west}),
        halo_copy(5, pack.at[pl.ds(2 * side - half, half)], (base + 2 * side, half), {"lat": lat + 1, "lon": east}),
    ]
    across = [
        halo_copy(6, pack.at[pl.ds(0, side)], (base + side, side), {"lon": west}),
        halo_copy(7, pack.at[pl.ds(side, side)], (base, side), {"lon": east}),
    ]

    @pl.when(has_n)
    def _():
        for copy in north:
            copy.start()

    @pl.when(has_s)
    def _():
        for copy in south:
            copy.start()

    for copy in across:
        copy.start()
    greet(relay.at[0])

    weights = [
        pltpu.make_async_remote_copy(
            src_ref=s, dst_ref=d, send_sem=weight_send.at[i], recv_sem=weight_recv.at[i],
            device_id=peer, device_id_type=MESH,
        )
        for i, (s, d) in enumerate(
            [
                (mw_h.at[0], mw.at[0, sub]), (nw_h.at[0], nw.at[0, sub]), (nb_h, nb.at[sub]),
                (no_h.at[0], no.at[0, sub]),
                (mw_h.at[1], mw.at[1, sub]), (nw_h.at[1], nw.at[1, sub]), (no_h.at[1], no.at[1, sub]),
            ]
        )
    ]
    for copy in weights:
        copy.start()

    @pl.when(jnp.logical_not(has_n))
    def _():
        halo[0:strip, :] = jnp.zeros((strip, halo.shape[1]), BF)
        halo[base + 2 * side:base + 2 * side + 2 * half, :] = jnp.zeros((2 * half, halo.shape[1]), BF)

    @pl.when(jnp.logical_not(has_s))
    def _():
        halo[strip:base, :] = jnp.zeros((strip, halo.shape[1]), BF)
        halo[base + 2 * side + 2 * half:base + 2 * side + 4 * half, :] = jnp.zeros(
            (2 * half, halo.shape[1]), BF
        )

    for i in range(2, 14):
        local[i].wait()
    table1[cells:cells + nodes, :] = dot(mesh[...], rw[0]).astype(BF)

    def weight_rows(layer):
        high, low = split(ew[layer])
        wf[0:4, :] = high
        wf[4:8, :] = high
        wf[8:12, :] = low
        high, low = split(eb[pl.ds(layer, 1), :])
        wf[12:13, :] = high
        wf[13:14, :] = low
        wf[14:16, :] = jnp.zeros((2, wf.shape[1]), F32)
        return wf[...].astype(BF)

    def feature_rows(fs, feat):
        high, low = split(feat[...])
        fs[0:4, :] = high
        fs[4:8, :] = low
        fs[8:12, :] = high
        fs[12:16, :] = jnp.ones((4, fs.shape[1]), F32)
        return fs[...].astype(BF)

    table1[cells + nodes:cells + nodes + FEAT_ROWS, :] = weight_rows(0)
    hot1[cells + nodes:cells + nodes + FEAT_ROWS, :] = feature_rows(fs1, feat1)

    def live(ids, which):
        slot = lax.broadcasted_iota(jnp.int32, ids.shape, 1)
        return jnp.where(slot < tiles[0:1, which:which + 1] * TILE, ids, -1)

    wide = gx + 2 * HALO
    place = snd1[...]
    r = place // wide
    c = place - r * wide
    rr, cc = r - HALO, c - HALO
    inside = (cc >= 0) & (cc < gx)
    edge_col = jnp.where(cc < 0, c, cc - gx)
    far_side = jnp.where(cc < 0, 0, 1)
    middle = jnp.where(inside, rr * gx + cc, cells + base + far_side * side + rr * HALO + edge_col)
    upper = jnp.where(inside, cells + r * gx + cc, cells + base + 2 * side + far_side * half + r * HALO + edge_col)
    down = rr - gy
    lower = jnp.where(
        inside,
        cells + strip + down * gx + cc,
        cells + base + 2 * side + (2 + far_side) * half + down * HALO + edge_col,
    )
    place = jnp.where(rr < 0, upper, jnp.where(rr >= gy, lower, middle))
    hot1[0:cells, :] = one_hot(place, cells)
    hot1h[...] = one_hot(place, hot1h.shape[0], cells)
    hot1[cells:cells + nodes, :] = one_hot(live(rcv1[...], 0), nodes)
    pre1[...] = dot_tn(table1[...], hot1[...])

    hot2f[...] = feature_rows(fs2, feat2)
    weights2 = weight_rows(1)
    rcv2[...] = live(rcv2[...], 1)
    span = min(SPAN, edges2)

    def select(step, carry):
        at = pl.ds(pl.multiple_of(step * span, span), span)
        ids = snd2[:, at]
        hot2[0:nodes, at] = one_hot(ids, nodes)
        hot2[nodes:2 * nodes, at] = one_hot(rcv2[:, at], nodes)
        source = (ids - nodes) // cap
        turn = me - source
        turn = jnp.where(turn < 0, turn + patches, turn)
        ids = jnp.where(ids < nodes, -1, turn * cap + (ids - nodes) - source * cap)
        hot2l[:, at] = one_hot(ids, patches * cap)
        pre2[:, at] = dot_tn(weights2, hot2f[:, at])
        return carry

    lax.fori_loop(0, edges2 // span, select, 0)

    def latent_part(latent, layer):
        for j in (0, 1):
            fixed[layer, j] = dot(latent, nw[layer, j, 0:latent.shape[1], :]) + nb[j, layer:layer + 1, :]

    def relayed(r):
        pl.semaphore_wait(relay.at[r], around)
        if r + 1 < rounds:
            greet(relay.at[r + 1])

    relayed(0)
    for i in range(14, len(local)):
        local[i].wait()
    for other in weights[:4]:
        other.wait()
    latent_part(mesh[...], 0)

    @pl.when(has_n)
    def _():
        for i in (3, 4, 5):
            south[i - 3].wait_recv()
        for copy in north:
            copy.wait_send()

    @pl.when(has_s)
    def _():
        for copy in north:
            copy.wait_recv()
        for copy in south:
            copy.wait_send()

    for copy in across:
        copy.wait()
    hidden = silu(pre1[...] + dot_tn(halo[...], hot1h[...])).astype(BF)

    def exchange(layer, total):
        sums[layer, sub] = total.astype(BF)
        copy = pltpu.make_async_remote_copy(
            src_ref=sums.at[layer, sub], dst_ref=sums.at[layer, sub], send_sem=sum_send.at[layer],
            recv_sem=sum_recv.at[layer], device_id=peer, device_id_type=MESH,
        )
        copy.start()
        return copy

    def node_update(latent, layer):
        inbound = dot(sums[layer, 0], mw[layer, 0]) + dot(sums[layer, 1], mw[layer, 1])
        inbound = inbound.astype(BF)
        total = 0.0
        for j in (0, 1):
            units = silu(fixed[layer, j] + dot(inbound, nw[layer, j, latent.shape[1]:, :])).astype(BF)
            total = total + dot(units, no[layer, j])
        return (latent.astype(F32) + layer_norm(total) * gain[layer:layer + 1, :]).astype(BF)

    copy = exchange(0, dot_nt(hot1[cells:cells + nodes, :], hidden))
    for r in range(1, rounds):
        relayed(r)
    copy.wait()
    mid = node_update(mesh[...], 0)

    sender = dot(mid, sw[1]).astype(BF)
    table2[0:nodes, :] = sender
    listed[...] = dot_tn(one_hot(lists[...], nodes), sender).reshape(listed.shape)
    routes = []
    for k in range(1, patches):
        q = lax.rem(me + k, patches)
        routes.append(
            pltpu.make_async_remote_copy(
                src_ref=listed.at[q], dst_ref=arrived.at[k], send_sem=list_send.at[k],
                recv_sem=list_recv.at[k], device_id={"lat": q // lons, "lon": lax.rem(q, lons)},
                device_id_type=MESH,
            )
        )
        routes[-1].start()
    arrived[0] = listed[me]
    table2[nodes:2 * nodes, :] = dot(mid, rw[1]).astype(BF)

    def before(step, carry):
        at = pl.ds(pl.multiple_of(step * span, span), span)
        pre2[:, at] += dot_tn(table2[...], hot2[:, at])
        return carry

    lax.fori_loop(0, edges2 // span, before, 0, unroll=True)
    for other in weights[4:]:
        other.wait()
    latent_part(mid, 1)
    for route in routes:
        route.wait()
    far = arrived[...].reshape(patches * cap, arrived.shape[2]).astype(BF)

    def after(step, total):
        at = pl.ds(pl.multiple_of(step * span, span), span)
        hidden = silu(pre2[:, at] + dot_tn(far, hot2l[:, at])).astype(BF)
        return total + dot_nt(hot2[nodes:2 * nodes, at], hidden)

    total = lax.fori_loop(0, edges2 // span, after, jnp.zeros((nodes, far.shape[1]), F32), unroll=True)
    exchange(1, total).wait()
    out_ref[...] = node_update(mid, 1)


def body(*args):
    (grid, mesh, snd1, rcv1, feat1, tiles, lists, snd2, rcv2, feat2,
     sw, rw, ew, eb, mw, nw, nb, no, gain) = args
    gy, gx, width = grid.shape
    bands, lons = lax.axis_size("lat"), lax.axis_size("lon")
    patches = bands * lons
    nodes = mesh.shape[0]
    units = sw.shape[2]
    cap = lists.shape[0] // patches
    edges1, edges2 = snd1.shape[0], snd2.shape[0]
    cells = gy * gx
    ring = (gy + 2 * HALO) * (gx + 2 * HALO) - cells
    operands = [
        grid.reshape(cells, width), mesh, snd1.reshape(1, -1), rcv1.reshape(1, -1), feat1,
        tiles.reshape(1, -1), lists.reshape(1, -1), snd2.reshape(1, -1), rcv2.reshape(1, -1), feat2,
        sw, rw, ew, eb, mw, nw, nb, no, gain,
    ]
    shapes = [op.shape for op in operands]
    for i in (14, 15, 17):
        shapes[i] = (shapes[i][0], 2) + shapes[i][1:]
    shapes[16] = (2,) + shapes[16]
    held = [pltpu.VMEM(shape, op.dtype) for shape, op in zip(shapes, operands)]
    dma = pltpu.SemaphoreType.DMA
    scratch = held + [
        pltpu.VMEM((cells + nodes + FEAT_ROWS, units), BF),
        pltpu.VMEM((ring, units), BF),
        pltpu.VMEM((2 * gy * HALO, units), BF),
        pltpu.VMEM((cells + nodes + FEAT_ROWS, edges1), BF),
        pltpu.VMEM((ring, edges1), BF),
        pltpu.VMEM((units, edges1), F32),
        pltpu.VMEM((FEAT_ROWS, edges1), F32),
        pltpu.VMEM((2 * nodes, units), BF),
        pltpu.VMEM((patches, cap, units), F32),
        pltpu.VMEM((patches, cap, units), F32),
        pltpu.VMEM((2 * nodes, edges2), BF),
        pltpu.VMEM((FEAT_ROWS, edges2), BF),
        pltpu.VMEM((patches * cap, edges2), BF),
        pltpu.VMEM((units, edges2), F32),
        pltpu.VMEM((FEAT_ROWS, edges2), F32),
        pltpu.VMEM((FEAT_ROWS, units), F32),
        pltpu.VMEM((2, 2, nodes, units), BF),
        pltpu.VMEM((2, 2, nodes, units), F32),
        pltpu.SemaphoreType.REGULAR((max(bands - 2, lons // 2 - 1),)),
        dma((24,)), dma((7,)), dma((7,)), dma((8,)), dma((8,)), dma((2,)), dma((2,)),
        dma((patches,)), dma((patches,)),
    ]
    return pl.pallas_call(
        functools.partial(kernel, (bands, lons, gy, gx, cap)),
        out_shape=jax.ShapeDtypeStruct(mesh.shape, mesh.dtype),
        in_specs=[pl.BlockSpec(memory_space=pltpu.HBM)] * len(operands),
        out_specs=pl.BlockSpec(memory_space=pltpu.VMEM),
        scratch_shapes=scratch,
        compiler_params=pltpu.CompilerParams(
            collective_id=0, has_side_effects=True, vmem_limit_bytes=58 * 1024 * 1024
        ),
        name="encoder_processor",
    )(*operands)


def solution(mesh):
    placed = (
        P(("member", "lat"), "lon", None),
        P(("member", "lat", "lon"), None),
        P(("lat", "lon")),
        P(("lat", "lon")),
        P(None, ("lat", "lon")),
        P(("lat", "lon")),
        P(("lat", "lon")),
        P(("lat", "lon")),
        P(("lat", "lon")),
        P(None, ("lat", "lon")),
        P(None, None, "sub"),
        P(None, None, "sub"),
        P(None, None, "sub"),
        P(None, "sub"),
        P(None, "sub", None),
        P(None, None, "sub"),
        P(None, "sub"),
        P(None, "sub", None),
        P(),
    )
    return jax.shard_map(
        body,
        mesh=mesh,
        in_specs=placed,
        out_specs=P(("member", "lat", "lon"), None),
        check_vma=False,
    )
```
